32 devices in a mesh: gx: 8 (over z, y), gz: 2 (over x), gy: 2 (over core).
Axes of the slice: x: 2, y: 2, z: 4, core: 2. Of those that a mesh axis runs over, the one named last changes fastest.
Arguments:
- field: bfloat16 [8, 192, 96, 256], P(None, 'gx', 'gz', 'gy'), may hold values from -25 to 25
- x_factor: bfloat16 [192, 48], P('gx'), may hold values from -0.4375 to 0.4375
- y_factor: bfloat16 [256, 48], P('gy'), may hold values from -0.375 to 0.375
- species_basis_matrix: float32 [8, 4], replicated, may hold values from -2 to 2
Outputs:
- gram: float32 [96, 96], P('gz')
The draws below stay inside these ranges and needn't reach their ends.
All inputs are finite; a program needn't handle non-finite values.
Results may differ from the reference program's by a relative error of at most 0.0003.
Values may be sent and summed in bfloat16 or wider, within the bound.
No kernel may reach another device: no remote copies, remote signals or barrier semaphores. Data moves between devices by JAX's collectives and lax.ppermute only.
A program may use at most 64 MiB of HBM per device.

```python
import math
import jax
import jax.numpy as jnp
from jax import lax

NS = 8
RX = 48
RY = 48
RS = 4
NX = 192
NY = 256
NZ = 96


def draw_field(key, part):
    key = jax.random.fold_in(key, 11)
    first, second, third = jax.random.split(key, 3)
    species_magnitude = jnp.exp(jax.random.uniform(first, (NS, 1, 1, 1), jnp.float32, math.log(0.7), math.log(1.4)))
    plane_magnitude = jnp.exp(jax.random.uniform(second, (1, 1, NZ, 1), jnp.float32, math.log(0.5), math.log(1.6)))
    values = jnp.clip(jax.random.normal(third, (NS, NX, NZ, NY), jnp.float32), -4.0, 4.0)
    return (species_magnitude * plane_magnitude * values).astype(jnp.bfloat16)


def block_scale(own_key, dims, pieces, smallest, largest):
    def one(axis_at, shards_of):
        heights = jax.random.uniform(jax.random.fold_in(jax.random.fold_in(own_key, 6), axis_at), (shards_of,), jnp.float32, smallest / len(pieces), largest / len(pieces))
        return jnp.repeat(jnp.exp(heights), dims[axis_at] // shards_of).reshape((-1,) + (1,) * (len(dims) - axis_at - 1))

    factor_of = one(*pieces[0])
    for cut in pieces[1:]:
        factor_of = factor_of * one(*cut)
    return factor_of


def gaussian(key, extent, deviation, reach, cuts=(), held_as=jnp.bfloat16):
    entries = deviation * jax.random.normal(key, extent, jnp.float32)
    if cuts:
        entries = entries * block_scale(key, extent, cuts, -0.22, 0.18)
    return jnp.clip(entries, -reach, reach).astype(held_as)


def setup_inputs(seed: int = 0) -> dict:
    seeds = jax.random.split(jax.random.key(seed), 5)
    field = draw_field(jax.random.fold_in(seeds[4], 71), 0)
    x_factor = gaussian(seeds[1], (NX, RX), NX ** -0.5, 0.4375, ((0, 8),))
    y_factor = gaussian(seeds[2], (NY, RY), NY ** -0.5, 0.375, ((0, 2),))
    species_basis_matrix = gaussian(seeds[3], (NS, RS), NS ** -0.5, 2.0, (), jnp.float32)
    return {"field": field, "x_factor": x_factor, "y_factor": y_factor, "species_basis_matrix": species_basis_matrix}


def reference(field, x_factor, y_factor, species_basis_matrix):
    def project(slab):
        flat = slab.reshape(-1, slab.shape[-1])
        product = jnp.dot(flat, y_factor, preferred_element_type=jnp.float32)
        return product.reshape(slab.shape[0], slab.shape[1], -1)

    across_y_axis = lax.map(project, field)
    reduced_tensor = jnp.einsum("sxzj,sp->pxzj", across_y_axis, species_basis_matrix.astype(jnp.float32), precision=lax.Precision.HIGHEST)
    core = jnp.einsum("xi,pxzj->zpji", x_factor.astype(jnp.float32), reduced_tensor, precision=lax.Precision.HIGHEST)
    unfolded = core.reshape(core.shape[0], -1)
    products = jnp.dot(unfolded, unfolded.T, precision=lax.Precision.HIGHEST)
    return products / (RX * RY * RS)
```

```python
import functools

import jax
import jax.numpy as jnp
from jax import lax
from jax.experimental import pallas as pl
from jax.experimental.pallas import tpu as pltpu
from jax.sharding import PartitionSpec as P

HIGHEST = lax.Precision.HIGHEST
F32 = jnp.float32
BF16 = jnp.bfloat16
LANES = 128
FETCH = 51
PAIR = 2
HEADROOM = 14.0
VMEM = pl.BlockSpec(memory_space=pltpu.VMEM)


EVERY = ("gy", "gz", "gx")


def place_of(gx, gz, gy, groups):
    return (gy * 2 + gz) * groups + gx


def limit(mib):
    return pltpu.CompilerParams(vmem_limit_bytes=mib * 1024 * 1024)


def iota(shape, axis):
    return lax.broadcasted_iota(jnp.int32, shape, axis)


def both_parts(value):
    high = value.astype(BF16)
    return high, (value - high.astype(F32)).astype(BF16)


def columns_of(shape, share, slot):
    lane = iota(shape, 1)
    owner, place = lax.shift_right_logical(lane, slot.bit_length() - 1), lane & (slot - 1)
    return owner * share + place, place < share


def spread_y(y_rows, share, slot):
    rank = y_rows.shape[0]
    column, used = columns_of((rank, LANES), share, slot)
    row = iota((rank, LANES), 0)
    pick = jnp.where(used & ((column == row) | (column == row + rank)), 1.0, 0.0).astype(BF16)
    return lax.dot_general(y_rows, pick, (((0,), (0,)), ((), ())), preferred_element_type=F32)


def weights_of(own, share, slot, rank, basis_ref, wide):
    cores = basis_ref.shape[0] // 2
    core = lax.axis_index("gy")
    of = core if own else cores - 1 - core
    rows = [jnp.where(of == 0, basis_ref[k : k + 1, :], basis_ref[2 + k : 3 + k, :]) for k in range(2)]
    second = columns_of((1, LANES), share, slot)[0] >= rank

    def weights(species):
        blocks = []
        for s in species:
            row = jnp.where(second, rows[1][:, s : s + 1], rows[0][:, s : s + 1])
            blocks.append(jnp.concatenate(both_parts(wide * row), axis=1))
        return jnp.concatenate(blocks, axis=0)

    return weights


def fetch_kernel(field_hbm, field_ref, sems):
    copies = []
    for k in range(field_ref.shape[0]):
        copies.append(pltpu.make_async_copy(field_hbm.at[k], field_ref.at[k], sems.at[k]))
        copies[-1].start()
    for copy in copies:
        copy.wait()


def fetch(field):
    return pl.pallas_call(
        fetch_kernel,
        in_specs=[pl.BlockSpec(memory_space=pltpu.HBM)],
        out_specs=VMEM,
        out_shape=jax.ShapeDtypeStruct(field.shape, field.dtype),
        scratch_shapes=[pltpu.SemaphoreType.DMA((field.shape[0],))],
        compiler_params=limit(FETCH),
    )(field)


def multiply(weights, field_ref, out_ref, sum_ref):
    species, breadth, planes, depth = field_ref.shape
    for k in range(0, species, PAIR):
        lhs = [field_ref[k + s].reshape(breadth * planes, depth) for s in range(PAIR)]
        held = weights(range(k, k + PAIR))
        both = jnp.dot(jnp.concatenate(lhs, axis=1), held, preferred_element_type=F32)
        if k > 0:
            both = both + sum_ref[...]
        if k + PAIR < species:
            sum_ref[...] = both
        else:
            out_ref[...] = both[:, :LANES] + both[:, LANES:]


def far_kernel(share, slot, basis_ref, y_ref, field_ref, out_ref, wide_ref, sum_ref):
    wide = spread_y(y_ref[...], share, slot)
    wide_ref[...] = wide
    multiply(weights_of(False, share, slot, y_ref.shape[0], basis_ref, wide), field_ref, out_ref, sum_ref)


def own_kernel(share, slot, rank, basis_ref, wide_ref, field_ref, out_ref, sum_ref):
    weights = weights_of(True, share, slot, rank, basis_ref, wide_ref[...])
    multiply(weights, field_ref, out_ref, sum_ref)


def project(kernel, basis_rows, y_values, field, more_out=()):
    _, breadth, planes, _ = field.shape
    out = [jax.ShapeDtypeStruct((breadth * planes, LANES), F32), *more_out]
    return pl.pallas_call(
        kernel,
        in_specs=[VMEM] * 3,
        out_specs=[VMEM] * len(out),
        out_shape=out,
        scratch_shapes=[pltpu.VMEM((breadth * planes, 2 * LANES), F32)],
        compiler_params=limit(32),
    )(basis_rows, y_values, field)


def exponent(value):
    largest = jnp.max(jnp.abs(value), axis=(0, 1), keepdims=True)
    return jnp.ceil(jnp.log2(jnp.maximum(largest, 2.0**-100)))


def trade(slot, owners, tiles):
    lane = iota(tiles[0].shape, 1)
    turned = [tile if z == 0 else pltpu.roll(tile, slot * z, 1) for z, tile in enumerate(tiles)]
    bit = 1
    while bit < owners:
        upper = (lane & (bit * slot)) != 0
        turned = [jnp.where(upper, turned[(n + bit) % owners], turned[n]) for n in range(owners)]
        bit *= 2
    picked = [turned[-k % owners] for k in range(owners)]
    return [tile if k == 0 else pltpu.roll(tile, LANES - slot * k, 1) for k, tile in enumerate(picked)]


def largest_of(ref):
    return jnp.max(jnp.abs(ref[...]).reshape(-1, 8, LANES), axis=0)


def trade_kernel(slot, mine_ref, x_ref, out_ref, largest_ref, ride_ref, power_ref):
    owners, breadth, width = out_ref.shape
    planes = width // slot
    rank = x_ref.shape[1]
    largest_ref[...] = largest_of(mine_ref)
    for g in range(planes // owners):
        rows = [pl.ds(g * owners + k, breadth, stride=planes) for k in range(owners)]
        for k, tile in enumerate(trade(slot, owners, [mine_ref[r, :] for r in rows])):
            out_ref[k, :, pl.ds(g * LANES, LANES)] = tile
    x_rows = x_ref[...].astype(F32)
    power = exponent(x_rows)
    x_rows = (x_rows * jnp.exp2(-power)).astype(BF16)
    place = jnp.where(iota((rank, width), 1) == iota((rank, width), 0) * slot + slot - 1, 1.0, 0.0)
    rides = jnp.dot(x_rows, place.astype(BF16), preferred_element_type=F32)
    turn = lax.axis_index("gz") * 2 + lax.axis_index("gy")
    part = rides[:8]
    for n in range(1, breadth // 8):
        part = jnp.where(turn == n, rides[8 * n : 8 * n + 8], part)
    ride_ref[...] = part
    power_ref[...] = jnp.broadcast_to(power, power_ref.shape)


def spread_own(mine, x_factor, slot):
    owners = LANES // slot
    breadth = x_factor.shape[0]
    planes = mine.shape[0] // breadth
    shapes = [(owners, breadth, planes * slot), (8, LANES), (8, planes * slot), (8, LANES)]
    return pl.pallas_call(
        functools.partial(trade_kernel, slot),
        in_specs=[VMEM] * 2,
        out_specs=[VMEM] * 4,
        out_shape=[jax.ShapeDtypeStruct(shape, F32) for shape in shapes],
        compiler_params=limit(32),
    )(mine, x_factor)


def pack(core, tiles, slot, share, x_tiles, powers):
    half, lane = share // 2, iota(tiles[0].shape, 1)
    place = lane & (slot - 1)
    packed = []
    for left, right in zip(tiles[0:-1:2], tiles[1:-1:2]):
        if core == 0:
            right = pltpu.roll(right, half, 1)
        else:
            left = pltpu.roll(left, LANES - half, 1)
        packed.append(jnp.where(place < half, left, right))
    for j in range(half):
        moved = pltpu.roll(tiles[-1], share - core * half - j, 1)
        packed[j] = jnp.where(place == share, moved, packed[j])
    for g, tile in enumerate(x_tiles):
        packed[g] = jnp.where(place == slot - 1, tile, packed[g])
    for n, power in enumerate(powers):
        packed[-1] = jnp.where(lane == n * slot + share, power, packed[-1])
    return packed


def unpack(packed, slot, share):
    half = share // 2
    place = iota(packed[0][0].shape, 1) & (slot - 1)
    tiles = []
    for first, second in zip(*packed):
        tiles.append(jnp.where(place < half, first, pltpu.roll(second, half, 1)))
        tiles.append(jnp.where(place < half, pltpu.roll(first, LANES - half, 1), second))
    last = jnp.zeros_like(tiles[0])
    for column in range(share):
        moved = pltpu.roll(packed[column // half][column % half], LANES - share + column, 1)
        last = jnp.where(place == column, moved, last)
    return tiles + [last]


def spread_kernel(slot, share, mine_ref, largest_ref, ride_ref, power_ref, other_ref, out_ref, sum_ref):
    owners, breadth, width = mine_ref.shape
    planes = width // slot
    power = exponent(largest_ref[...] + largest_of(other_ref))
    factor = jnp.exp2(HEADROOM - power)
    x_tiles = [ride_ref[:, pl.ds(c, LANES)] for c in range(0, width, LANES)]
    for g in range(planes // owners):
        rows = [pl.ds(g * owners + k, breadth, stride=planes) for k in range(owners)]
        lanes = pl.ds(g * LANES, LANES)
        for k, tile in enumerate(trade(slot, owners, [other_ref[r, :] for r in rows])):
            sum_ref[k, :, lanes] = (mine_ref[k, :, lanes] + tile) * factor
    for k in range(owners):
        tiles = [
            sum_ref[k, pl.ds(r, 8), pl.ds(c, LANES)]
            for r in range(0, breadth, 8)
            for c in range(0, width, LANES)
        ]
        for core in range(2):
            for t, tile in enumerate(pack(core, tiles, slot, share, x_tiles, (power, power_ref[...]))):
                out_ref[place_of(k // 2, k % 2, core, owners // 2), pl.ds(8 * t, 8), :] = tile


def spread(mine, other, slot, share):
    owners, breadth, width = mine[0].shape
    return pl.pallas_call(
        functools.partial(spread_kernel, slot, share),
        in_specs=[VMEM] * 5,
        out_specs=VMEM,
        out_shape=jax.ShapeDtypeStruct((2 * owners, breadth * width // LANES // 16 * 8, LANES), F32),
        scratch_shapes=[pltpu.VMEM(mine[0].shape, F32)],
        compiler_params=limit(32),
    )(*mine, other)


def gram_kernel(groups, share, slot, scale, parts_ref, out_ref, core_ref, rows_ref, wide_ref, factor_ref):
    senders, height, _ = parts_ref.shape
    blocks = senders // groups // 2
    width = core_ref.shape[0] // blocks
    planes = width // slot
    rank = core_ref.shape[1]
    across = width // LANES
    take = jnp.where(iota((width, rank), 0) == iota((width, rank), 1) * slot + slot - 1, 1.0, 0.0)
    take = take.astype(BF16)
    is_x = (iota((8, LANES), 1) & (slot - 1)) == slot - 1
    for d in range(senders):
        factor_ref[pl.ds(d, 1), :] = parts_ref[d, pl.ds(height - 8, 1), :]
    rows = factor_ref[...]
    lane = iota(rows.shape, 1)
    powers = jnp.where(lane == slot + share, jnp.exp2(rows), 0.0)
    powers = jnp.where(lane == share, jnp.exp2(rows - HEADROOM), powers)
    lane, row = iota((LANES, LANES), 1) & (slot - 1), iota((LANES, LANES), 0)
    given = jnp.where(lane == slot - 1, slot + share, share)
    spread_to = jnp.where(row == given, 1.0, 0.0).astype(BF16)
    factor_ref[...] = jnp.dot(powers.astype(BF16), spread_to, preferred_element_type=F32)
    chunks = [[] for _ in range(blocks)]
    for g in range(groups):
        packed = []
        for s in range(2 * blocks):
            at = place_of(g, s // 2, s % 2, groups)
            factor = factor_ref[pl.ds(at, 1), :]
            packed.append([parts_ref[at, pl.ds(r, 8), :] * factor for r in range(0, height, 8)])
        for b in range(blocks):
            tiles = unpack(packed[2 * b : 2 * b + 2], slot, share)
            if b == 0:
                for t in range(len(tiles)):
                    tiles[t] = jnp.where(is_x, packed[t // across][t % across], tiles[t])
            for t in range(0, len(tiles), across):
                chunks[b].append(jnp.concatenate(tiles[t : t + across], axis=1))
    x_all = None
    for b in range(blocks):
        high, low = both_parts(jnp.concatenate(chunks[b], axis=0))
        if x_all is None:
            x_all = jnp.dot(high, take, preferred_element_type=F32).astype(BF16)
        dims = (((0,), (0,)), ((), ()))
        core = lax.dot_general(high, x_all, dims, preferred_element_type=F32)
        core = core + lax.dot_general(low, x_all, dims, preferred_element_type=F32)
        core_ref[pl.ds(b * width, width), :] = core
    rows_ref[...] = jnp.zeros_like(rows_ref)
    for c in range(share):
        for b in range(blocks):
            rows = core_ref[pl.ds(b * width + c, planes, stride=slot), :]
            rows_ref[pl.ds(b * planes, planes), pl.ds(c * LANES, rank)] = rows
    high, low = both_parts(rows_ref[...])
    dims = (((1,), (1,)), ((), ()))
    cross = lax.dot_general(high, low, dims, preferred_element_type=F32)
    gram = lax.dot_general(high, high, dims, preferred_element_type=F32)
    gram = (gram + cross + cross.T) * scale
    power = exponent(gram)
    wide_ref[...] = jnp.broadcast_to(power, wide_ref.shape)
    wide_ref[:, : blocks * planes] = gram * jnp.exp2(HEADROOM - power)
    copies, height, _ = out_ref.shape
    wide = [wide_ref[pl.ds(start, height), :] for start in range(0, blocks * planes, height)]
    for d in range(copies):
        out_ref[d] = wide[d // groups % 2 * 2 + d // groups // 2]


def gram_rows(parts, groups, planes, rank, share, slot, scale):
    blocks = parts.shape[0] // groups // 2
    width = planes * slot
    return pl.pallas_call(
        functools.partial(gram_kernel, groups, share, slot, scale),
        in_specs=[VMEM],
        out_specs=VMEM,
        out_shape=jax.ShapeDtypeStruct((parts.shape[0], planes // 2, LANES), F32),
        scratch_shapes=[
            pltpu.VMEM((blocks * width, rank), F32),
            pltpu.VMEM((blocks * planes, share * LANES), F32),
            pltpu.VMEM((blocks * planes, LANES), F32),
            pltpu.VMEM((parts.shape[0], LANES), F32),
        ],
        compiler_params=limit(32),
    )(parts)


def sum_kernel(parts_ref, out_ref):
    width = out_ref.shape[1]
    total = 0.0
    for d in range(parts_ref.shape[0]):
        power = parts_ref[d, :, width : width + 1]
        total = total + parts_ref[d, :, :width] * jnp.exp2(power - HEADROOM)
    out_ref[...] = total


def sum_parts(parts, width):
    return pl.pallas_call(
        sum_kernel,
        in_specs=[VMEM],
        out_specs=VMEM,
        out_shape=jax.ShapeDtypeStruct((parts.shape[1], width), F32),
        compiler_params=limit(32),
    )(parts)


def join_kernel(own_ref, other_ref, out_ref):
    first = lax.axis_index("gy") == 0
    half = own_ref.shape[0]
    out_ref[:half] = jnp.where(first, own_ref[...], other_ref[...])
    out_ref[half:] = jnp.where(first, other_ref[...], own_ref[...])


def join(own, other):
    return pl.pallas_call(
        join_kernel,
        in_specs=[VMEM] * 2,
        out_specs=VMEM,
        out_shape=jax.ShapeDtypeStruct((2 * own.shape[0], own.shape[1]), F32),
        compiler_params=limit(32),
    )(own, other)


def swap_with_all(value, axes):
    return lax.all_to_all(value, axes, split_axis=0, concat_axis=0, tiled=True)


def swap_cores(value):
    return lax.ppermute(value, "gy", [(0, 1), (1, 0)])


def fast_body(field, x_factor, y_factor, species_basis_matrix):
    planes = field.shape[2]
    first_rank, second_rank = x_factor.shape[1], y_factor.shape[1]
    target_rank = species_basis_matrix.shape[1]
    gx, gz, gy = (lax.axis_size(name) for name in ("gx", "gz", "gy"))
    owners = gx * gz
    slot = LANES // owners
    share = target_rank * second_rank // (owners * gy)
    y_rows, basis_rows = y_factor.T, species_basis_matrix.T
    held = fetch(field)
    far, wide = project(
        functools.partial(far_kernel, share, slot),
        basis_rows,
        y_rows,
        held,
        [jax.ShapeDtypeStruct((y_rows.shape[1], LANES), F32)],
    )
    other = swap_cores(far)
    (mine,) = project(functools.partial(own_kernel, share, slot, second_rank), basis_rows, wide, held)
    chunks = spread(spread_own(mine, x_factor, slot), other, slot, share)
    parts = swap_with_all(chunks.astype(jnp.float16), EVERY).astype(F32)
    scale = 1.0 / (first_rank * second_rank * target_rank)
    rows = gram_rows(parts, gx, planes, first_rank, share, slot, scale)
    rows = swap_with_all(rows.astype(jnp.float16), EVERY).astype(F32)
    rows = sum_parts(rows, gz * planes)
    return join(rows, swap_cores(rows))


def any_body(field, x_factor, y_factor, species_basis_matrix):
    species_count, breadth, planes, depth = field.shape
    first_rank = x_factor.shape[1]
    second_rank = y_factor.shape[1]
    target_rank = species_basis_matrix.shape[1]
    gx, gz, gy = (lax.axis_size(name) for name in ("gx", "gz", "gy"))
    z_at, y_at = lax.axis_index("gz"), lax.axis_index("gy")
    flat = field.reshape(species_count * breadth * planes, depth)
    across_y = lax.dot_general(
        y_factor, flat, (((0,), (1,)), ((), ())), preferred_element_type=F32
    ).reshape(second_rank, species_count, breadth * planes)
    reduced = jnp.einsum("qtb,tf->fqb", across_y, species_basis_matrix, precision=HIGHEST)
    reduced = reduced.reshape(target_rank * second_rank, breadth, planes)
    half = reduced.shape[0] // gy
    mine = lax.dynamic_slice_in_dim(reduced, y_at * half, half, 0)
    for step in range(1, gy):
        other = lax.dynamic_slice_in_dim(reduced, lax.rem(y_at + step, gy) * half, half, 0)
        mine = mine + lax.ppermute(other, "gy", [(i, (i + step) % gy) for i in range(gy)])
    group = gx * gz
    share = -(-half // group)
    mine = jnp.pad(mine, ((0, share * group - half), (0, 0), (0, 0)))
    whole_x = lax.all_gather(x_factor, "gx", axis=0, tiled=True).astype(F32)
    parts = swap_with_all(mine.reshape(group, share, breadth, planes), ("gx", "gz"))
    parts = parts.reshape(gx, gz, share, breadth, planes)
    core = jnp.einsum("asi,abpsz->bzpi", whole_x.reshape(gx, breadth, first_rank), parts, precision=HIGHEST)
    core = core.reshape(gz * planes, share * first_rank)
    gram = lax.dot_general(core, core, (((1,), (1,)), ((), ())), precision=HIGHEST)
    gram = lax.psum_scatter(gram, "gz", scatter_dimension=0, tiled=True)
    return lax.psum(gram, ("gx", "gy")) / (first_rank * second_rank * target_rank)


def body(field, x_factor, y_factor, species_basis_matrix):
    _, breadth, planes, depth = field.shape
    gx, gz, gy = (lax.axis_size(name) for name in ("gx", "gz", "gy"))
    owners = gx * gz
    columns = species_basis_matrix.shape[1] * y_factor.shape[1]
    fits = (
        gx > 1
        and gy == 2
        and gz == 2
        and owners == 16
        and columns == 6 * owners * gy
        and species_basis_matrix.shape[1] == 2 * gy
        and breadth == 24
        and planes == 3 * owners
        and planes == x_factor.shape[1]
        and field.shape[0] % PAIR == 0
        and depth == LANES
    )
    return (fast_body if fits else any_body)(field, x_factor, y_factor, species_basis_matrix)


def solution(mesh):
    placed = (P(None, "gx", "gz", "gy"), P("gx", None), P("gy", None), P())
    return jax.shard_map(body, mesh=mesh, in_specs=placed, out_specs=P("gz", None), check_vma=False)
```
